512 devices in a mesh: seq: 64 (over y_hi, z, core), dp: 8 (over y_lo, x).
Axes of the slice: x: 4, y: 4 (y_hi: 2, y_lo: 2; y = y_hi * 2 + y_lo), z: 16, core: 2. Of those that a mesh axis runs over, the one named last changes fastest.
Arguments:
- queries: bfloat16 [65536, 768], P(('dp', 'seq')), parts along dimension 0, may hold values from -6.5 to 6.5, as said below
- key_states: bfloat16 [65536, 768], P(('dp', 'seq')), parts along dimension 0, may hold values from -6.5 to 6.5, as said below
- value_states: bfloat16 [65536, 768], P(('dp', 'seq')), parts along dimension 0, may hold values from -6 to 6
- grad_output: bfloat16 [65536, 768], P(('dp', 'seq')), parts along dimension 0, may hold values from -6 to 6
- head_offsets: int32 [4, 12], replicated, may hold values from 0 to 63, as said below
Outputs:
- attended: bfloat16 [65536, 768], P(('dp', 'seq')), parts along dimension 0
- grad_queries: bfloat16 [65536, 768], P(('dp', 'seq')), parts along dimension 0
- grad_keys: bfloat16 [65536, 768], P(('dp', 'seq')), parts along dimension 0
- grad_values: bfloat16 [65536, 768], P(('dp', 'seq')), parts along dimension 0
The draws below stay inside these ranges and needn't reach their ends.
There are 8 independent parts, one for each index of `dp`. The reference program is written for one: setup_inputs(seed, part) draws one part's arguments, and reference() takes and returns one part's arrays. A program takes and returns all parts, laid end to end along the dimension named above; an argument that names none is the same for every part. Nothing has to cross between parts.
Inputs may be any that keep to these rules, and one draw needn't show every extreme that they name: `queries`: float entries, hot rows included. `key_states`: float entries, hot rows included. head_offsets[l, h] lies in 0 to g - 1 for level l's group size g (1, 4, 16, 64); at every level some head takes g - 1.
All inputs are finite; a program needn't handle non-finite values.
Results may differ from the reference program's by a relative error of at most 0.025.
Values may be sent and summed in bfloat16 or wider, within the bound.
No kernel may reach another device: no remote copies, remote signals or barrier semaphores. Data moves between devices by JAX's collectives and lax.ppermute only.
A program may use at most 64 MiB of HBM per device.

```python
import jax
import jax.numpy as jnp
from jax import lax

HEADS = 12
HEAD_DIM = 64
TOK_DEV = 128
LEVELS = 4
D = 768
SEQ = 8192
N_SEQ = 64


def draw_queries(key, part):
    key = jax.random.fold_in(key, 1)
    values = jnp.clip(jax.random.normal(key, (TOK_DEV * N_SEQ, HEADS * HEAD_DIM)), -4.5, 4.5)
    return values.astype(jnp.bfloat16)


def draw_key_states(key, part):
    key = jax.random.fold_in(key, 3)
    values = jnp.clip(jax.random.normal(key, (TOK_DEV * N_SEQ, HEADS * HEAD_DIM)), -4.5, 4.5)
    return values.astype(jnp.bfloat16)


def draw_head_offsets(key, part):
    key = jax.random.fold_in(key, 5)
    groups = jnp.array([1, 4, N_SEQ // 4, N_SEQ], dtype=jnp.int32)
    values = jax.random.randint(key, (LEVELS, HEADS), 0, groups[:, None], dtype=jnp.int32)
    pick_key = jax.random.fold_in(key, 6)
    chosen = jax.random.randint(pick_key, (LEVELS, 1), 0, HEADS, dtype=jnp.int32)
    heads_index = jnp.arange(HEADS, dtype=jnp.int32)[None, :]
    return jnp.where(heads_index == chosen, groups[:, None] - 1, values)


def levels(rng, shape, cuts, low, top_value):
    def one(dim, blocks):
        heights = jax.random.uniform(jax.random.fold_in(jax.random.fold_in(rng, 6), dim), (blocks,), jnp.float32, low / len(cuts), top_value / len(cuts))
        return jnp.repeat(jnp.exp(heights), shape[dim] // blocks).reshape((-1,) + (1,) * (len(shape) - dim - 1))

    gain = one(*cuts[0])
    for cut in cuts[1:]:
        gain = gain * one(*cut)
    return gain


def bell_draw(own_key, shape, scale, bound, cuts=(), kind=jnp.bfloat16):
    loudness = levels(own_key, shape, cuts, -0.22, 0.18) if cuts else 1.0
    entries = jax.random.normal(own_key, shape, jnp.float32) * scale * loudness
    return jnp.minimum(jnp.maximum(entries, -bound), bound).astype(kind)


def setup_inputs(seed: int = 0, part: int = 0) -> dict:
    key_list = jax.random.split(jax.random.key(seed), 6)
    part_splits = jax.random.split(jax.random.fold_in(key_list[5], part), 6)
    return {
        "queries": draw_queries(jax.random.fold_in(jax.random.fold_in(key_list[5], part), 71), part),
        "key_states": draw_key_states(jax.random.fold_in(jax.random.fold_in(key_list[5], part), 71), part),
        "value_states": bell_draw(part_splits[2], (SEQ, D), 1.0, 6.0, ((0, 64),)),
        "grad_output": bell_draw(part_splits[3], (SEQ, D), 1.0, 6.0, ((0, 64),)),
        "head_offsets": draw_head_offsets(jax.random.fold_in(key_list[5], 71), part),
    }


NEG_FILL = -1.0e30


def pick_rows(source, group, offset_row):
    rows, heads, width = source.shape
    shaped = source.reshape(rows // group, group, heads, width)
    onehot = jnp.arange(group, dtype=jnp.int32)[:, None] == offset_row[None, :].astype(jnp.int32)
    return jnp.sum(jnp.where(onehot[None, :, :, None], shaped, jnp.zeros((), source.dtype)), axis=1)


def place_rows(picked, group, offset_row, fill):
    rows, heads, width = picked.shape
    onehot = jnp.arange(group, dtype=jnp.int32)[:, None] == offset_row[None, :].astype(jnp.int32)
    spread = jnp.where(onehot[None, :, :, None], picked[:, None, :, :], jnp.asarray(fill, picked.dtype))
    return spread.reshape(rows * group, heads, width)


def pair_scores(query_sel, key_all):
    scale = HEAD_DIM ** -0.5
    return jnp.einsum("qhd,khd->hqk", query_sel.astype(jnp.float32), key_all.astype(jnp.float32)) * scale


def attend(query_sel, key_all, value_all):
    scores = pair_scores(query_sel, key_all)
    level_max = jnp.max(scores, axis=-1)
    raw = jnp.exp(scores - level_max[..., None])
    level_total = jnp.sum(raw, axis=-1)
    weights = lax.optimization_barrier(raw.astype(jnp.bfloat16)).astype(jnp.float32)
    level_sum = jnp.einsum("hqk,khd->qhd", weights, value_all.astype(jnp.float32))
    return level_max.T, level_total.T, level_sum


def attend_back(query_sel, grad_sel, log_sel, delta_sel, key_all, value_all):
    scale = HEAD_DIM ** -0.5
    scores = pair_scores(query_sel, key_all)
    probs = jnp.exp(scores - log_sel.T[:, :, None])
    grad_probs = jnp.einsum("qhd,khd->hqk", grad_sel.astype(jnp.float32), value_all.astype(jnp.float32))
    grad_scores = probs * (grad_probs - delta_sel.T[:, :, None])
    low_scores = lax.optimization_barrier(grad_scores.astype(jnp.bfloat16)).astype(jnp.float32)
    low_probs = lax.optimization_barrier(probs.astype(jnp.bfloat16)).astype(jnp.float32)
    grad_value = jnp.einsum("hqk,qhd->khd", low_probs, grad_sel.astype(jnp.float32))
    grad_key = jnp.einsum("hqk,qhd->khd", low_scores, query_sel.astype(jnp.float32)) * scale
    grad_query = jnp.einsum("hqk,khd->qhd", low_scores, key_all.astype(jnp.float32)) * scale
    return grad_query, grad_key, grad_value


def reference(queries, key_states, value_states, grad_output, head_offsets):
    seq_len = queries.shape[0]
    groups = (1, 4, N_SEQ // 4, N_SEQ)
    query3 = queries.reshape(seq_len, HEADS, HEAD_DIM)
    key3 = key_states.reshape(seq_len, HEADS, HEAD_DIM)
    value3 = value_states.reshape(seq_len, HEADS, HEAD_DIM)
    grad3 = grad_output.reshape(seq_len, HEADS, HEAD_DIM)

    def segments(source, group, offset_row):
        picked = pick_rows(source, group, offset_row)
        return picked.reshape(N_SEQ // group, TOK_DEV, HEADS, source.shape[2])

    stats = []
    for level in range(4):
        group = groups[level]
        offset_row = head_offsets[level]
        parts = (segments(query3, group, offset_row), segments(key3, group, offset_row), segments(value3, group, offset_row))

        def segment_forward(items):
            return attend(items[0], items[1], items[2])

        level_max, level_total, level_sum = lax.map(segment_forward, parts)
        rows = seq_len // group
        stats.append((
            place_rows(level_max.reshape(rows, HEADS, 1), group, offset_row, NEG_FILL)[..., 0],
            place_rows(level_total.reshape(rows, HEADS, 1), group, offset_row, 0.0)[..., 0],
            place_rows(level_sum.reshape(rows, HEADS, HEAD_DIM), group, offset_row, 0.0)))

    top_max = stats[0][0]
    for item in stats[1:]:
        top_max = jnp.maximum(top_max, item[0])
    total = jnp.zeros_like(top_max)
    combined = jnp.zeros((seq_len, HEADS, HEAD_DIM), jnp.float32)
    for item in stats:
        factor = jnp.exp(item[0] - top_max)
        total = total + factor * item[1]
        combined = combined + factor[..., None] * item[2]
    attended3 = (combined / total[..., None]).astype(jnp.bfloat16)
    log_total = top_max + jnp.log(total)
    delta = jnp.sum(grad3.astype(jnp.float32) * attended3.astype(jnp.float32), axis=-1)

    grad_query = jnp.zeros((seq_len, HEADS, HEAD_DIM), jnp.float32)
    grad_key = jnp.zeros((seq_len, HEADS, HEAD_DIM), jnp.float32)
    grad_value = jnp.zeros((seq_len, HEADS, HEAD_DIM), jnp.float32)
    for level in range(4):
        group = groups[level]
        offset_row = head_offsets[level]
        parts = (segments(query3, group, offset_row), segments(grad3, group, offset_row),
                 segments(log_total[..., None], group, offset_row)[..., 0],
                 segments(delta[..., None], group, offset_row)[..., 0],
                 segments(key3, group, offset_row), segments(value3, group, offset_row))

        def segment_back(items):
            return attend_back(items[0], items[1], items[2], items[3], items[4], items[5])

        query_part, key_part, value_part = lax.map(segment_back, parts)
        rows = seq_len // group
        grad_query = grad_query + place_rows(query_part.reshape(rows, HEADS, HEAD_DIM), group, offset_row, 0.0)
        grad_key = grad_key + place_rows(key_part.reshape(rows, HEADS, HEAD_DIM), group, offset_row, 0.0)
        grad_value = grad_value + place_rows(value_part.reshape(rows, HEADS, HEAD_DIM), group, offset_row, 0.0)

    width = HEADS * HEAD_DIM
    return (attended3.reshape(seq_len, width),
            grad_query.reshape(seq_len, width).astype(jnp.bfloat16),
            grad_key.reshape(seq_len, width).astype(jnp.bfloat16),
            grad_value.reshape(seq_len, width).astype(jnp.bfloat16))
```

```python
import functools

import jax
import jax.numpy as jnp
from jax import lax
from jax.experimental import pallas as pl
from jax.experimental.pallas import tpu as pltpu
from jax.sharding import Mesh, PartitionSpec as P

HEADS = 12
WIDTH = 64
TOK = 128
FULL = HEADS * WIDTH
PAIRS = HEADS // 2
SCALE = WIDTH ** -0.5
GROUPS = (1, 4, 16, 64)
PARTS = (("yh", 2), ("zh", 2), ("zm", 4), ("zl", 2), ("c", 2))
FAR = ("yh", "zh", "zm")
NEAR = ("zl", "c")
N_FAR = 16
N_NEAR = 4
ROWS1, ROWS2, ROWS3 = 32, 8, 2
NEG = -1e30
F32 = jnp.float32
BF16 = jnp.bfloat16
VMEM = pl.BlockSpec(memory_space=pltpu.VMEM)
SMEM = pl.BlockSpec(memory_space=pltpu.SMEM)
PARAMS = pltpu.CompilerParams(vmem_limit_bytes=48 * 1024 * 1024)


def iota(shape, dim):
    return lax.broadcasted_iota(jnp.int32, shape, dim)


def dot(a, b):
    return lax.dot_general(a, b, (((1,), (0,)), ((), ())), preferred_element_type=F32)


def dot_t(a, b):
    return lax.dot_general(a, b, (((1,), (1,)), ((), ())), preferred_element_type=F32)


def lanes(pair):
    return slice(pair * 128, (pair + 1) * 128)


def halves(value):
    n = value.shape[0] // 2
    return jnp.where(iota((n, 128), 1) < WIDTH, value[:n], value[n:])


def stacked(value):
    low = iota(value.shape, 1) < WIDTH
    zero = jnp.zeros_like(value)
    return jnp.concatenate([jnp.where(low, value, zero), jnp.where(low, zero, value)], 0)


def pick_kernel(off_ref, k_ref, v_ref, q_ref, g_ref, near_ref, mid_ref, far_ref):
    refs = (k_ref, v_ref, q_ref, g_ref)
    row = iota((48, TOK), 0)
    tok = iota((48, TOK), 1)
    base = jnp.where(row < 32, row * 4, jnp.where(row < 40, (row - 32) * 16, (row % 2) * 64))

    def selector(head, array):
        off = jnp.where(
            row < 32, off_ref[1, head], jnp.where(row < 40, off_ref[2, head], off_ref[3, head])
        )
        live = (row < 40) | ((row - 40) // 2 == array)
        return jnp.where((tok == base + off) & live, 1.0, 0.0).astype(BF16)

    for pair in range(PAIRS):
        picked = []
        for array in range(4):
            choose = jnp.concatenate(
                [selector(2 * pair, array), selector(2 * pair + 1, array)], 0
            )
            picked.append(halves(dot(choose, refs[array][:, lanes(pair)])))
        near_ref[:, lanes(pair)] = jnp.concatenate([x[:32] for x in picked], 0).astype(BF16)
        mid_ref[:, lanes(pair)] = jnp.concatenate([x[32:40] for x in picked], 0).astype(BF16)
        far = picked[0][40:] + picked[1][40:] + picked[2][40:] + picked[3][40:]
        far_ref[:, lanes(pair)] = far.astype(BF16)


def split_kernel(far_ref, mid_ref, kv_ref, qg_ref):
    both = jnp.concatenate([far_ref[...], mid_ref[...]], 0)
    row = iota((128, 256), 0)
    col = iota((128, 256), 1)
    run = row // 32
    slot = row % 32
    for first, out_ref in ((0, kv_ref), (2, qg_ref)):
        array = first + run // 2
        far_col = slot // 2 * 8 + array * 2 + slot % 2
        mid_col = 128 + slot // 8 * 32 + array * 8 + slot % 8
        choose = jnp.where(col == jnp.where(run % 2 == 0, far_col, mid_col), 1.0, 0.0)
        out_ref[...] = dot(choose.astype(BF16), both).astype(BF16)


def gathered(own_ref, near_ref, back_ref, array, pair):
    cols = lanes(pair)
    one = [near_ref[d * 128 + array * 32 : d * 128 + array * 32 + 32, cols] for d in range(N_NEAR)]
    half = (array % 2) * 64
    three = [back_ref[d * 128 + half : d * 128 + half + 32, cols] for d in range(N_NEAR)]
    two = [back_ref[d * 128 + half + 32 : d * 128 + half + 64, cols] for d in range(N_NEAR)]
    return jnp.concatenate([own_ref[:, cols]] + one + two + three, 0)


def chosen(off_ref, head, level):
    return (iota((TOK, 1), 0) & (GROUPS[level] - 1)) == off_ref[level, head]


def forward_kernel(
    off_ref, k_ref, v_ref, q_ref, g_ref, near_ref, back_ref, att_ref, gq_ref, stat_ref, own_ref
):
    tok = iota((TOK, 128), 0)
    lane = iota((1, 128), 1)
    eye = tok == iota((TOK, 128), 1)
    sums = [None] * 8
    for pair in range(PAIRS):
        keys = gathered(k_ref, near_ref, back_ref, 0, pair)
        values = gathered(v_ref, near_ref, back_ref, 1, pair)
        grad = stacked(g_ref[:, lanes(pair)])
        scores = dot_t(stacked(q_ref[:, lanes(pair)]), keys) * SCALE
        live = [
            jnp.concatenate(
                [chosen(off_ref, 2 * pair, level), chosen(off_ref, 2 * pair + 1, level)], 0
            )
            for level in range(1, 4)
        ]
        blocks = [scores[:, level * 128 : level * 128 + 128] for level in range(4)]
        top = blocks[0]
        for level in range(1, 4):
            top = jnp.maximum(top, jnp.where(live[level - 1], blocks[level], NEG))
        top = jnp.max(top, axis=1, keepdims=True)
        raw = [jnp.exp(blocks[0] - top)]
        for level in range(1, 4):
            raw.append(jnp.exp(blocks[level] - jnp.where(live[level - 1], top, -NEG)))
        total = jnp.sum(raw[0] + raw[1] + raw[2] + raw[3], axis=1, keepdims=True)
        inverse = 1.0 / total
        raw = jnp.concatenate(raw, 1)
        out = halves(dot(raw.astype(BF16), values) * inverse).astype(BF16)
        att_ref[:, lanes(pair)] = out
        out = out.astype(F32)
        delta = jnp.sum(grad.astype(F32) * jnp.concatenate([out, out], 0), axis=1, keepdims=True)
        grad_probs = dot_t(grad, values)
        grad_scores = (raw * inverse * (grad_probs - delta)).astype(BF16)
        gq_ref[:, lanes(pair)] = halves(dot(grad_scores, keys) * SCALE).astype(BF16)
        logs = top + jnp.log(total)
        for side in range(2):
            head = 2 * pair + side
            turn = head // 4
            one = lane - 32 * turn
            two = lane - 96 - 8 * turn
            three = lane - 120 - 2 * turn
            source = jnp.where(
                (one >= 0) & (one < 32),
                one * 4 + off_ref[1, head],
                jnp.where(
                    (two >= 0) & (two < 8),
                    two * 16 + off_ref[2, head],
                    jnp.where(
                        (three >= 0) & (three < 2), three * 64 + off_ref[3, head], -1
                    ),
                ),
            )
            hit = tok == source
            for kind, column in enumerate((logs, delta)):
                column = column[side * TOK : side * TOK + TOK]
                own_ref[2 * head + kind : 2 * head + kind + 1, :] = jnp.sum(
                    jnp.where(eye, column, 0.0), axis=0, keepdims=True
                )
                line = jnp.sum(jnp.where(hit, column, 0.0), axis=0, keepdims=True)
                place = 2 * (head % 4) + kind
                sums[place] = line if sums[place] is None else sums[place] + line
    stat_ref[...] = jnp.concatenate(sums, 0)


def backward_kernel(
    off_ref, where_ref, k_ref, v_ref, q_ref, g_ref, near_ref, back_ref, own_ref, stat_ref,
    gk_ref, gv_ref, line_ref,
):
    lane = iota((8, 128), 1)
    mine = where_ref[0]

    def block(d, peer):
        return stat_ref[pl.ds(pl.multiple_of((d * N_FAR + peer) * 8, 8), 8), :]

    zero = jnp.zeros((8, 128), F32)
    acc = [[zero] * 3 for _ in range(3)]

    def put(level, value, at, width, start):
        inside = (lane >= at) & (lane < at + width)
        for turn in range(3):
            moved = pltpu.roll(value, (at - start - width * turn) % 128, 1)
            acc[level][turn] = jnp.where(inside, moved, acc[level][turn])

    for d in range(N_NEAR):
        put(0, block(d, mine), d * 32, 32, 0)
        for slot, step in enumerate((0, 2, 1, 3)):
            put(1, block(d, mine ^ step), d * 32 + slot * 8, 8, 96)
        for peer in range(N_FAR):
            put(2, block(d, peer), d * 32 + peer * 2, 2, 120)
    for level in range(3):
        for turn in range(3):
            line_ref[turn * 8 : turn * 8 + 8, level * 128 : level * 128 + 128] = acc[level][turn]

    for pair in range(PAIRS):
        queries = gathered(q_ref, near_ref, back_ref, 2, pair)
        grads = gathered(g_ref, near_ref, back_ref, 3, pair)
        scores = dot_t(stacked(k_ref[:, lanes(pair)]), queries) * SCALE
        grad_probs = dot_t(stacked(v_ref[:, lanes(pair)]), grads)
        probs, grad_scores = [], []
        for side in range(2):
            head = 2 * pair + side
            rows = slice(side * TOK, side * TOK + TOK)
            probs_row, grad_row = [], []
            for level in range(4):
                cols = slice(level * 128, level * 128 + 128)
                if level == 0:
                    log_line = own_ref[2 * head : 2 * head + 1, :]
                    delta_line = own_ref[2 * head + 1 : 2 * head + 2, :]
                else:
                    at = slice(level * 128 - 128, level * 128)
                    log_line = line_ref[2 * head : 2 * head + 1, at]
                    delta_line = line_ref[2 * head + 1 : 2 * head + 2, at]
                power = scores[rows, cols] - log_line
                if level:
                    power = jnp.where(chosen(off_ref, head, level), power, NEG)
                prob = jnp.exp(power)
                probs_row.append(prob.astype(BF16))
                grad_row.append((prob * (grad_probs[rows, cols] - delta_line)).astype(BF16))
            probs.append(jnp.concatenate(probs_row, 1))
            grad_scores.append(jnp.concatenate(grad_row, 1))
        gv_ref[:, lanes(pair)] = halves(dot(jnp.concatenate(probs, 0), grads)).astype(BF16)
        gk_ref[:, lanes(pair)] = halves(
            dot(jnp.concatenate(grad_scores, 0), queries) * SCALE
        ).astype(BF16)


def shape(*dims, dtype=BF16):
    return jax.ShapeDtypeStruct(dims, dtype)


def cost(flops, moved, exps=0):
    return pl.CostEstimate(flops=flops, bytes_accessed=moved, transcendentals=exps)


def to_far(value):
    rows, cols = value.shape
    spread = jnp.broadcast_to(value[None], (N_FAR, rows, cols)).reshape(N_FAR * rows, cols)
    return lax.all_to_all(spread, FAR, 0, 0, tiled=True)


def to_near(value):
    return lax.all_gather(value, NEAR, axis=0, tiled=True)


def swap_mid(value, step):
    return lax.ppermute(value, "zm", [(i, i ^ step) for i in range(4)])


def on_device(queries, key_states, value_states, grad_output, head_offsets):
    mine = (lax.axis_index("yh") * 2 + lax.axis_index("zh")) * 4 + lax.axis_index("zm")
    own = (key_states, value_states, queries, grad_output)
    near, mid, far = pl.pallas_call(
        pick_kernel,
        name="pick",
        out_shape=(shape(128, FULL), shape(32, FULL), shape(8, FULL)),
        in_specs=[SMEM] + [VMEM] * 4,
        out_specs=(VMEM,) * 3,
        compiler_params=PARAMS,
        cost_estimate=cost(200_000_000, 1_100_000),
    )(head_offsets, *own)
    far_rows = to_far(far)
    mid_rows = jnp.concatenate([mid, swap_mid(mid, 2)], 0)
    mid_rows = jnp.concatenate([mid_rows, swap_mid(mid_rows, 1)], 0)
    near_rows = to_near(near)
    kv_rows, qg_rows = pl.pallas_call(
        split_kernel,
        name="split",
        out_shape=(shape(128, FULL), shape(128, FULL)),
        in_specs=[VMEM] * 2,
        out_specs=(VMEM,) * 2,
        compiler_params=PARAMS,
        cost_estimate=cost(100_000_000, 800_000),
    )(far_rows, mid_rows)
    kv_rows = to_near(kv_rows)
    attended, grad_query, stats, own_stats = pl.pallas_call(
        forward_kernel,
        name="forward",
        out_shape=(
            shape(TOK, FULL),
            shape(TOK, FULL),
            shape(8, 128, dtype=F32),
            shape(2 * HEADS, 128, dtype=F32),
        ),
        in_specs=[SMEM] + [VMEM] * 6,
        out_specs=(VMEM,) * 4,
        compiler_params=PARAMS,
        cost_estimate=cost(1_000_000_000, 3_000_000, 800_000),
    )(head_offsets, *own, near_rows, kv_rows)
    all_stats = to_near(to_far(stats))
    qg_rows = to_near(qg_rows)
    grad_key, grad_value = pl.pallas_call(
        backward_kernel,
        name="backward",
        out_shape=(shape(TOK, FULL), shape(TOK, FULL)),
        in_specs=[SMEM] * 2 + [VMEM] * 8,
        out_specs=(VMEM,) * 2,
        scratch_shapes=[pltpu.VMEM((2 * HEADS, 3 * 128), F32)],
        compiler_params=PARAMS,
        cost_estimate=cost(1_000_000_000, 3_000_000, 800_000),
    )(head_offsets, mine.reshape(1), *own, near_rows, qg_rows, own_stats, all_stats)
    return attended, grad_query, grad_key, grad_value


def solution(mesh):
    names = tuple(name for name, _ in PARTS)
    sizes = tuple(size for _, size in PARTS)
    parts = Mesh(mesh.devices.reshape(sizes + mesh.devices.shape[1:]), names + ("dp",))
    rows = P(("dp",) + names, None)
    return jax.shard_map(
        on_device,
        mesh=parts,
        in_specs=(rows,) * 4 + (P(),),
        out_specs=(rows,) * 4,
        check_vma=False,
    )
```

```python
import functools

import jax
import jax.numpy as jnp
from jax import lax
from jax.experimental import pallas as pl
from jax.experimental.pallas import tpu as pltpu
from jax.sharding import Mesh, PartitionSpec as P

HEADS = 12
WIDTH = 64
TOK = 128
FULL = HEADS * WIDTH
PAIRS = HEADS // 2
SCALE = WIDTH ** -0.5
GROUPS = (1, 4, 16, 64)
PARTS = (("yh", 2), ("zh", 2), ("zm", 4), ("zl", 2), ("c", 2))
FAR = ("yh", "zh", "zm")
NEAR = ("zl", "c")
N_FAR = 16
N_NEAR = 4
ROWS1, ROWS2, ROWS3 = 32, 8, 2
NEG = -1e30
CUTS = 4
F32 = jnp.float32
BF16 = jnp.bfloat16
VMEM = pl.BlockSpec(memory_space=pltpu.VMEM)
SMEM = pl.BlockSpec(memory_space=pltpu.SMEM)
PARAMS = pltpu.CompilerParams(vmem_limit_bytes=48 * 1024 * 1024)


def iota(shape, dim):
    return lax.broadcasted_iota(jnp.int32, shape, dim)


def dot(a, b):
    return lax.dot_general(a, b, (((1,), (0,)), ((), ())), preferred_element_type=F32)


def dot_t(a, b):
    return lax.dot_general(a, b, (((1,), (1,)), ((), ())), preferred_element_type=F32)


def lanes(pair):
    return slice(pair * 128, (pair + 1) * 128)


def halves(value):
    n = value.shape[0] // 2
    return jnp.where(iota((n, 128), 1) < WIDTH, value[:n], value[n:])


def stacked(value):
    low = iota(value.shape, 1) < WIDTH
    zero = jnp.zeros_like(value)
    return jnp.concatenate([jnp.where(low, value, zero), jnp.where(low, zero, value)], 0)


def pick_kernel(off_ref, k_hbm, v_hbm, q_hbm, g_hbm, near_ref, mid_ref, far_ref, refs, sems):
    copies = []
    for array, source in enumerate((k_hbm, v_hbm, q_hbm, g_hbm)):
        for part in range(CUTS):
            rows = pl.ds(part * (TOK // CUTS), TOK // CUTS)
            copies.append(
                pltpu.make_async_copy(
                    source.at[rows], refs.at[array, rows], sems.at[array, part]
                )
            )
    for copy in copies:
        copy.start()
    row = iota((48, TOK), 0)
    tok = iota((48, TOK), 1)
    base = jnp.where(row < 32, row * 4, jnp.where(row < 40, (row - 32) * 16, (row % 2) * 64))

    def selector(head, array):
        off = jnp.where(
            row < 32, off_ref[1, head], jnp.where(row < 40, off_ref[2, head], off_ref[3, head])
        )
        live = (row < 40) | ((row - 40) // 2 == array)
        return jnp.where((tok == base + off) & live, 1.0, 0.0).astype(BF16)

    far = [None] * PAIRS
    for first in (0, 2):
        for copy in copies[first * CUTS : (first + 2) * CUTS]:
            copy.wait()
        for pair in range(PAIRS):
            picked = []
            for array in (first, first + 1):
                choose = jnp.concatenate(
                    [selector(2 * pair, array), selector(2 * pair + 1, array)], 0
                )
                picked.append(halves(dot(choose, refs[array, :, lanes(pair)])))
            near_ref[first * 32 : first * 32 + 64, lanes(pair)] = jnp.concatenate(
                [x[:32] for x in picked], 0
            ).astype(BF16)
            mid_ref[first * 8 : first * 8 + 16, lanes(pair)] = jnp.concatenate(
                [x[32:40] for x in picked], 0
            ).astype(BF16)
            both = picked[0][40:] + picked[1][40:]
            far[pair] = both if far[pair] is None else far[pair] + both
    for pair in range(PAIRS):
        far_ref[:, lanes(pair)] = jnp.concatenate([far[pair]] * N_FAR, 0).astype(BF16)


def split_kernel(far_ref, mid_ref, kv_ref, qg_ref):
    both = jnp.concatenate([far_ref[...], mid_ref[...]], 0)
    row = iota((128, 256), 0)
    col = iota((128, 256), 1)
    run = row // 32
    slot = row % 32
    for first, out_ref in ((0, kv_ref), (2, qg_ref)):
        array = first + run // 2
        far_col = slot // 2 * 8 + array * 2 + slot % 2
        mid_col = 128 + slot // 8 * 32 + array * 8 + slot % 8
        choose = jnp.where(col == jnp.where(run % 2 == 0, far_col, mid_col), 1.0, 0.0)
        out_ref[...] = dot(choose.astype(BF16), both).astype(BF16)


def gathered(own_ref, near_ref, back_ref, array, pair):
    cols = lanes(pair)
    one = [near_ref[d * 128 + array * 32 : d * 128 + array * 32 + 32, cols] for d in range(N_NEAR)]
    half = (array % 2) * 64
    three = [back_ref[d * 128 + half : d * 128 + half + 32, cols] for d in range(N_NEAR)]
    two = [back_ref[d * 128 + half + 32 : d * 128 + half + 64, cols] for d in range(N_NEAR)]
    return jnp.concatenate([own_ref[:, cols]] + one + two + three, 0)


def chosen(off_ref, pair, level, tok):
    half = tok.shape[0] // 2
    off = jnp.where(
        iota(tok.shape, 0) < half, off_ref[level, 2 * pair], off_ref[level, 2 * pair + 1]
    )
    return (tok & (GROUPS[level] - 1)) == off


def softmax(scores, live):
    blocks = [scores[:, level * 128 : level * 128 + 128] for level in range(4)]
    for level in range(1, 4):
        blocks[level] = jnp.where(live[level - 1], blocks[level], NEG)
    top = jnp.maximum(jnp.maximum(blocks[0], blocks[1]), jnp.maximum(blocks[2], blocks[3]))
    top = jnp.max(top, axis=1, keepdims=True)
    raw = [jnp.exp(block - top) for block in blocks]
    total = jnp.sum((raw[0] + raw[1]) + (raw[2] + raw[3]), axis=1, keepdims=True)
    return jnp.concatenate(raw, 1), total, top


def stat_kernel(
    off_ref, k_ref, v_ref, near_ref, mid_ref, far_ref, near_rows_ref, back_ref, stat_ref
):
    row = iota((48, 1), 0)
    both = iota((96, 128), 0)
    slot = jnp.where(both < 48, both, both - 48)
    sums = [None] * 8

    def pick(level, pair):
        return jnp.where(both < 48, off_ref[level, 2 * pair], off_ref[level, 2 * pair + 1])

    for pair in range(PAIRS):
        cols = lanes(pair)
        far = far_ref[:16, cols].astype(F32)[:8]
        mid = mid_ref[16:, cols].astype(F32)
        near = near_ref[64:, cols].astype(F32)
        query = jnp.concatenate([near[:32], mid[:8], pltpu.roll(far, 4, 0)], 0).astype(BF16)
        grad = stacked(jnp.concatenate([near[32:], mid[8:], pltpu.roll(far, 2, 0)], 0))
        keys = gathered(k_ref, near_rows_ref, back_ref, 0, pair)
        values = gathered(v_ref, near_rows_ref, back_ref, 1, pair)
        tok = jnp.where(
            slot < 32,
            slot * 4 + pick(1, pair),
            jnp.where(slot < 40, (slot - 32) * 16 + pick(2, pair), slot % 2 * 64 + pick(3, pair)),
        )
        live = [chosen(off_ref, pair, level, tok) for level in range(1, 4)]
        raw, total, top = softmax(dot_t(stacked(query), keys) * SCALE, live)
        out = (dot(raw.astype(BF16), values) * (1.0 / total)).astype(BF16).astype(F32)
        delta = jnp.sum(grad * out, axis=1, keepdims=True)
        logs = top + jnp.log(total)
        turn = pair // 2
        lane = jnp.where(
            row < 32,
            row + 32 * turn,
            jnp.where(
                row < 40, row + 64 + 8 * turn, jnp.where(row < 42, row + 80 + 2 * turn, -1)
            ),
        )
        hit = iota((48, 128), 1) == lane
        for side in range(2):
            for kind, column in enumerate((logs, delta)):
                line = jnp.sum(
                    jnp.where(hit, column[side * 48 : side * 48 + 48], 0.0), axis=0, keepdims=True
                )
                place = 2 * ((2 * pair + side) % 4) + kind
                sums[place] = line if sums[place] is None else sums[place] + line
    stat_ref[...] = jnp.concatenate(sums * N_FAR, 0)


def forward_kernel(
    off_ref, k_ref, v_ref, q_ref, g_ref, near_ref, back_ref, att_ref, gq_ref, own_ref
):
    eye = iota((TOK, 128), 0) == iota((TOK, 128), 1)
    row = iota((2 * TOK, 128), 0)
    for pair in range(PAIRS):
        keys = gathered(k_ref, near_ref, back_ref, 0, pair)
        values = gathered(v_ref, near_ref, back_ref, 1, pair)
        grad = stacked(g_ref[:, lanes(pair)])
        scores = dot_t(stacked(q_ref[:, lanes(pair)]), keys) * SCALE
        live = [chosen(off_ref, pair, level, row) for level in range(1, 4)]
        raw, total, top = softmax(scores, live)
        inverse = 1.0 / total
        out = halves(dot(raw.astype(BF16), values) * inverse).astype(BF16)
        att_ref[:, lanes(pair)] = out
        out = out.astype(F32)
        delta = jnp.sum(grad.astype(F32) * jnp.concatenate([out, out], 0), axis=1, keepdims=True)
        grad_probs = dot_t(grad, values)
        grad_scores = (raw * inverse * (grad_probs - delta)).astype(BF16)
        gq_ref[:, lanes(pair)] = halves(dot(grad_scores, keys) * SCALE).astype(BF16)
        logs = top + jnp.log(total)
        for side in range(2):
            head = 2 * pair + side
            for kind, column in enumerate((logs, delta)):
                own_ref[2 * head + kind : 2 * head + kind + 1, :] = jnp.sum(
                    jnp.where(eye, column[side * TOK : side * TOK + TOK], 0.0),
                    axis=0,
                    keepdims=True,
                )


def backward_kernel(
    off_ref, where_ref, k_ref, v_ref, q_ref, g_ref, near_ref, back_ref, own_ref, stat_ref,
    gk_ref, gv_ref, line_ref,
):
    lane = iota((8, 128), 1)
    row = iota((2 * TOK, 128), 0)
    mine = where_ref[0]
    side = where_ref[1] * 2

    def block(d, peer):
        return stat_ref[pl.ds(pl.multiple_of((d * N_FAR + peer) * 8, 8), 8), :]

    zero = jnp.zeros((8, 128), F32)
    acc = [[zero] * 3 for _ in range(3)]

    def put(level, value, at, width, start):
        inside = (lane >= at) & (lane < at + width)
        for turn in range(3):
            moved = pltpu.roll(value, (at - start - width * turn) % 128, 1)
            acc[level][turn] = jnp.where(inside, moved, acc[level][turn])

    for at in range(N_NEAR):
        d = (at % 2 * 2) ^ side | at // 2
        put(0, block(d, mine), at * 32, 32, 0)
        for slot, step in enumerate((0, 2, 1, 3)):
            put(1, block(d, mine ^ step), at * 32 + slot * 8, 8, 96)
        for peer in range(N_FAR):
            put(2, block(d, peer), at * 32 + peer * 2, 2, 120)
    for level in range(3):
        for turn in range(3):
            line_ref[turn * 8 : turn * 8 + 8, level * 128 : level * 128 + 128] = acc[level][turn]

    for pair in range(PAIRS):
        queries = gathered(q_ref, near_ref, back_ref, 2, pair)
        grads = gathered(g_ref, near_ref, back_ref, 3, pair)
        scores = dot_t(stacked(k_ref[:, lanes(pair)]), queries) * SCALE
        grad_probs = dot_t(stacked(v_ref[:, lanes(pair)]), grads)
        live = [None] + [chosen(off_ref, pair, level, row) for level in range(1, 4)]
        probs, grad_scores = [], []
        for side in range(2):
            head = 2 * pair + side
            rows = slice(side * TOK, side * TOK + TOK)
            probs_row, grad_row = [], []
            for level in range(4):
                cols = slice(level * 128, level * 128 + 128)
                if level == 0:
                    log_line = own_ref[2 * head : 2 * head + 1, :]
                    delta_line = own_ref[2 * head + 1 : 2 * head + 2, :]
                else:
                    at = slice(level * 128 - 128, level * 128)
                    log_line = line_ref[2 * head : 2 * head + 1, at]
                    delta_line = line_ref[2 * head + 1 : 2 * head + 2, at]
                power = scores[rows, cols] - log_line
                if level:
                    power = jnp.where(live[level][rows], power, NEG)
                prob = jnp.exp(power)
                probs_row.append(prob.astype(BF16))
                grad_row.append((prob * (grad_probs[rows, cols] - delta_line)).astype(BF16))
            probs.append(jnp.concatenate(probs_row, 1))
            grad_scores.append(jnp.concatenate(grad_row, 1))
        gv_ref[:, lanes(pair)] = halves(dot(jnp.concatenate(probs, 0), grads)).astype(BF16)
        gk_ref[:, lanes(pair)] = halves(
            dot(jnp.concatenate(grad_scores, 0), queries) * SCALE
        ).astype(BF16)


def shape(*dims, dtype=BF16):
    return jax.ShapeDtypeStruct(dims, dtype)


def cost(flops, moved, exps=0):
    return pl.CostEstimate(flops=flops, bytes_accessed=moved, transcendentals=exps)


def to_far(value):
    return lax.all_to_all(value, FAR, 0, 0, tiled=True)


def to_near(value):
    return lax.all_gather(value, NEAR, axis=0, tiled=True)


def to_pair(value):
    other = lax.ppermute(value, "zl", [(0, 1), (1, 0)])
    return lax.all_gather(jnp.concatenate([value, other], 0), "c", axis=0, tiled=True)


def swap_mid(value, step):
    return lax.ppermute(value, "zm", [(i, i ^ step) for i in range(4)])


def on_device(queries, key_states, value_states, grad_output, head_offsets):
    mine = (lax.axis_index("yh") * 2 + lax.axis_index("zh")) * 4 + lax.axis_index("zm")
    place = jnp.stack([mine, lax.axis_index("zl")])
    own = (key_states, value_states, queries, grad_output)
    near, mid, far = pl.pallas_call(
        pick_kernel,
        name="pick",
        out_shape=(shape(128, FULL), shape(32, FULL), shape(8 * N_FAR, FULL)),
        in_specs=[SMEM] + [pl.BlockSpec(memory_space=pl.ANY)] * 4,
        out_specs=(VMEM,) * 3,
        scratch_shapes=[pltpu.VMEM((4, TOK, FULL), BF16), pltpu.SemaphoreType.DMA((4, CUTS))],
        compiler_params=pltpu.CompilerParams(vmem_limit_bytes=62 * 1024 * 1024),
        cost_estimate=cost(200_000_000, 1_100_000),
    )(head_offsets, *own)
    far_rows = to_far(far)
    mid_rows = jnp.concatenate([mid, swap_mid(mid, 2), swap_mid(mid, 1), swap_mid(mid, 3)], 0)
    near_rows = to_pair(near)
    kv_rows, qg_rows = pl.pallas_call(
        split_kernel,
        name="split",
        out_shape=(shape(128, FULL), shape(128, FULL)),
        in_specs=[VMEM] * 2,
        out_specs=(VMEM,) * 2,
        compiler_params=PARAMS,
        cost_estimate=cost(100_000_000, 800_000),
    )(far_rows, mid_rows)
    kv_rows = to_pair(kv_rows)
    stats = pl.pallas_call(
        stat_kernel,
        name="stats",
        out_shape=shape(8 * N_FAR, 128, dtype=F32),
        in_specs=[SMEM] + [VMEM] * 7,
        out_specs=VMEM,
        compiler_params=PARAMS,
        cost_estimate=cost(200_000_000, 2_000_000, 300_000),
    )(head_offsets, key_states, value_states, near, mid, far, near_rows, kv_rows)
    attended, grad_query, own_stats = pl.pallas_call(
        forward_kernel,
        name="forward",
        out_shape=(
            shape(TOK, FULL),
            shape(TOK, FULL),
            shape(2 * HEADS, 128, dtype=F32),
        ),
        in_specs=[SMEM] + [VMEM] * 6,
        out_specs=(VMEM,) * 3,
        compiler_params=PARAMS,
        cost_estimate=cost(1_000_000_000, 3_000_000, 800_000),
    )(head_offsets, *own, near_rows, kv_rows)
    all_stats = to_near(to_far(stats))
    qg_rows = to_pair(qg_rows)
    grad_key, grad_value = pl.pallas_call(
        backward_kernel,
        name="backward",
        out_shape=(shape(TOK, FULL), shape(TOK, FULL)),
        in_specs=[SMEM] * 2 + [VMEM] * 8,
        out_specs=(VMEM,) * 2,
        scratch_shapes=[pltpu.VMEM((2 * HEADS, 3 * 128), F32)],
        compiler_params=PARAMS,
        cost_estimate=cost(1_000_000_000, 3_000_000, 800_000),
    )(head_offsets, place, *own, near_rows, qg_rows, own_stats, all_stats)
    return attended, grad_query, grad_key, grad_value


def solution(mesh):
    names = tuple(name for name, _ in PARTS)
    sizes = tuple(size for _, size in PARTS)
    parts = Mesh(mesh.devices.reshape(sizes + mesh.devices.shape[1:]), names + ("dp",))
    rows = P(("dp",) + names, None)
    return jax.shard_map(
        on_device,
        mesh=parts,
        in_specs=(rows,) * 4 + (P(),),
        out_specs=(rows,) * 4,
        check_vma=False,
    )
```

```python
import functools

import jax
import jax.numpy as jnp
from jax import lax
from jax.experimental import pallas as pl
from jax.experimental.pallas import tpu as pltpu
from jax.sharding import Mesh, PartitionSpec as P

HEADS = 12
WIDTH = 64
TOK = 128
FULL = HEADS * WIDTH
PAIRS = HEADS // 2
SCALE = WIDTH ** -0.5
GROUPS = (1, 4, 16, 64)
PARTS = (("yh", 2), ("zh", 2), ("zm", 4), ("zl", 2), ("c", 2))
FAR = ("yh", "zh", "zm")
NEAR = ("zl", "c")
N_FAR = 16
N_NEAR = 4
ROWS1, ROWS2, ROWS3 = 32, 8, 2
NEG = -1e30
CUTS = 4
ROOT_ROWS, ROOT_STATS = 13, 2
F32 = jnp.float32
BF16 = jnp.bfloat16
VMEM = pl.BlockSpec(memory_space=pltpu.VMEM)
SMEM = pl.BlockSpec(memory_space=pltpu.SMEM)
PARAMS = pltpu.CompilerParams(vmem_limit_bytes=48 * 1024 * 1024)


def iota(shape, dim):
    return lax.broadcasted_iota(jnp.int32, shape, dim)


def dot(a, b):
    return lax.dot_general(a, b, (((1,), (0,)), ((), ())), preferred_element_type=F32)


def dot_t(a, b):
    return lax.dot_general(a, b, (((1,), (1,)), ((), ())), preferred_element_type=F32)


def lanes(pair):
    return slice(pair * 128, (pair + 1) * 128)


def halves(value):
    n = value.shape[0] // 2
    return jnp.where(iota((n, 128), 1) < WIDTH, value[:n], value[n:])


def stacked(value):
    low = iota(value.shape, 1) < WIDTH
    zero = jnp.zeros_like(value)
    return jnp.concatenate([jnp.where(low, value, zero), jnp.where(low, zero, value)], 0)


def pick_kernel(off_ref, k_hbm, v_hbm, q_hbm, g_hbm, near_ref, mid_ref, far_ref, refs, sems):
    copies = []
    for array, source in enumerate((k_hbm, v_hbm, q_hbm, g_hbm)):
        for part in range(CUTS):
            rows = pl.ds(part * (TOK // CUTS), TOK // CUTS)
            copies.append(
                pltpu.make_async_copy(
                    source.at[rows], refs.at[array, rows], sems.at[array, part]
                )
            )
    for copy in copies:
        copy.start()
    row = iota((48, TOK), 0)
    tok = iota((48, TOK), 1)
    base = jnp.where(row < 32, row * 4, jnp.where(row < 40, (row - 32) * 16, (row % 2) * 64))

    def selector(head, array):
        off = jnp.where(
            row < 32, off_ref[1, head], jnp.where(row < 40, off_ref[2, head], off_ref[3, head])
        )
        live = (row < 40) | ((row - 40) // 2 == array)
        return jnp.where((tok == base + off) & live, 1.0, 0.0).astype(BF16)

    far = [None] * PAIRS
    for first in (0, 2):
        for copy in copies[first * CUTS : (first + 2) * CUTS]:
            copy.wait()
        for pair in range(PAIRS):
            picked = []
            for array in (first, first + 1):
                choose = jnp.concatenate(
                    [selector(2 * pair, array), selector(2 * pair + 1, array)], 0
                )
                picked.append(halves(dot(choose, refs[array, :, lanes(pair)])))
            near_ref[first * 32 : first * 32 + 64, lanes(pair)] = jnp.concatenate(
                [x[:32] for x in picked], 0
            ).astype(BF16)
            mid_ref[first * 8 : first * 8 + 16, lanes(pair)] = jnp.concatenate(
                [x[32:40] for x in picked], 0
            ).astype(BF16)
            both = picked[0][40:] + picked[1][40:]
            far[pair] = both if far[pair] is None else far[pair] + both
    for pair in range(PAIRS):
        far_ref[:, lanes(pair)] = jnp.concatenate([far[pair]] * N_FAR, 0).astype(BF16)


def split_kernel(far_ref, mid_ref, q_ref, g_ref, kv_ref, qg_ref):
    del q_ref, g_ref
    both = jnp.concatenate([far_ref[...], mid_ref[...]], 0)
    row = iota((128, 256), 0)
    col = iota((128, 256), 1)
    run = row // 32
    slot = row % 32
    for first, out_ref in ((0, kv_ref), (2, qg_ref)):
        array = first + run // 2
        far_col = slot // 2 * 8 + array * 2 + slot % 2
        mid_col = 128 + slot // 8 * 32 + array * 8 + slot % 8
        choose = jnp.where(col == jnp.where(run % 2 == 0, far_col, mid_col), 1.0, 0.0)
        out_ref[...] = dot(choose.astype(BF16), both).astype(BF16)


def gathered(own_ref, near_ref, back_ref, array, pair):
    cols = lanes(pair)
    one = [near_ref[d * 128 + array * 32 : d * 128 + array * 32 + 32, cols] for d in range(N_NEAR)]
    half = (array % 2) * 64
    three = [back_ref[d * 128 + half : d * 128 + half + 32, cols] for d in range(N_NEAR)]
    two = [back_ref[d * 128 + half + 32 : d * 128 + half + 64, cols] for d in range(N_NEAR)]
    return jnp.concatenate([own_ref[:, cols]] + one + two + three, 0)


def chosen(off_ref, pair, level, tok):
    half = tok.shape[0] // 2
    off = jnp.where(
        iota(tok.shape, 0) < half, off_ref[level, 2 * pair], off_ref[level, 2 * pair + 1]
    )
    return (tok & (GROUPS[level] - 1)) == off


def softmax(scores, live):
    blocks = [scores[:, level * 128 : level * 128 + 128] for level in range(4)]
    for level in range(1, 4):
        blocks[level] = jnp.where(live[level - 1], blocks[level], NEG)
    top = jnp.maximum(jnp.maximum(blocks[0], blocks[1]), jnp.maximum(blocks[2], blocks[3]))
    top = jnp.max(top, axis=1, keepdims=True)
    raw = [jnp.exp(block - top) for block in blocks]
    total = jnp.sum((raw[0] + raw[1]) + (raw[2] + raw[3]), axis=1, keepdims=True)
    return jnp.concatenate(raw, 1), total, top


def stat_kernel(
    off_ref, k_ref, v_ref, near_ref, mid_ref, far_ref, near_rows_ref, back_ref, stat_ref
):
    row = iota((48, 1), 0)
    both = iota((96, 128), 0)
    slot = jnp.where(both < 48, both, both - 48)
    sums = [None] * 8

    def pick(level, pair):
        return jnp.where(both < 48, off_ref[level, 2 * pair], off_ref[level, 2 * pair + 1])

    for pair in range(PAIRS):
        cols = lanes(pair)
        far = far_ref[:16, cols].astype(F32)[:8]
        mid = mid_ref[16:, cols].astype(F32)
        near = near_ref[64:, cols].astype(F32)
        query = jnp.concatenate([near[:32], mid[:8], pltpu.roll(far, 4, 0)], 0).astype(BF16)
        grad = stacked(jnp.concatenate([near[32:], mid[8:], pltpu.roll(far, 2, 0)], 0))
        keys = gathered(k_ref, near_rows_ref, back_ref, 0, pair)
        values = gathered(v_ref, near_rows_ref, back_ref, 1, pair)
        tok = jnp.where(
            slot < 32,
            slot * 4 + pick(1, pair),
            jnp.where(slot < 40, (slot - 32) * 16 + pick(2, pair), slot % 2 * 64 + pick(3, pair)),
        )
        live = [chosen(off_ref, pair, level, tok) for level in range(1, 4)]
        raw, total, top = softmax(dot_t(stacked(query), keys) * SCALE, live)
        out = (dot(raw.astype(BF16), values) * (1.0 / total)).astype(BF16).astype(F32)
        delta = jnp.sum(grad * out, axis=1, keepdims=True)
        logs = top + jnp.log(total)
        turn = pair // 2
        lane = jnp.where(
            row < 32,
            row + 32 * turn,
            jnp.where(
                row < 40, row + 64 + 8 * turn, jnp.where(row < 42, row + 80 + 2 * turn, -1)
            ),
        )
        hit = iota((48, 128), 1) == lane
        for side in range(2):
            for kind, column in enumerate((logs, delta)):
                line = jnp.sum(
                    jnp.where(hit, column[side * 48 : side * 48 + 48], 0.0), axis=0, keepdims=True
                )
                place = 2 * ((2 * pair + side) % 4) + kind
                sums[place] = line if sums[place] is None else sums[place] + line
    stat_ref[...] = jnp.concatenate(sums * N_FAR, 0)


def forward_kernel(
    off_ref, k_ref, v_ref, q_ref, g_ref, near_ref, back_ref, att_ref, gq_ref, own_ref
):
    eye = iota((TOK, 128), 0) == iota((TOK, 128), 1)
    row = iota((2 * TOK, 128), 0)
    for pair in range(PAIRS):
        keys = gathered(k_ref, near_ref, back_ref, 0, pair)
        values = gathered(v_ref, near_ref, back_ref, 1, pair)
        grad = stacked(g_ref[:, lanes(pair)])
        scores = dot_t(stacked(q_ref[:, lanes(pair)]), keys) * SCALE
        live = [chosen(off_ref, pair, level, row) for level in range(1, 4)]
        raw, total, top = softmax(scores, live)
        inverse = 1.0 / total
        out = halves(dot(raw.astype(BF16), values) * inverse).astype(BF16)
        att_ref[:, lanes(pair)] = out
        out = out.astype(F32)
        delta = jnp.sum(grad.astype(F32) * jnp.concatenate([out, out], 0), axis=1, keepdims=True)
        grad_probs = dot_t(grad, values)
        grad_scores = (raw * inverse * (grad_probs - delta)).astype(BF16)
        gq_ref[:, lanes(pair)] = halves(dot(grad_scores, keys) * SCALE).astype(BF16)
        logs = top + jnp.log(total)
        for side in range(2):
            head = 2 * pair + side
            for kind, column in enumerate((logs, delta)):
                own_ref[2 * head + kind : 2 * head + kind + 1, :] = jnp.sum(
                    jnp.where(eye, column[side * TOK : side * TOK + TOK], 0.0),
                    axis=0,
                    keepdims=True,
                )


def backward_kernel(
    off_ref, where_ref, k_ref, v_ref, q_ref, g_ref, near_ref, back_ref, own_ref, stat_ref,
    gk_ref, gv_ref, line_ref,
):
    lane = iota((8, 128), 1)
    row = iota((2 * TOK, 128), 0)
    mine = where_ref[0]
    side = where_ref[1] * 2

    def block(d, peer):
        return stat_ref[pl.ds(pl.multiple_of((d * N_FAR + (peer ^ ROOT_STATS)) * 8, 8), 8), :]

    zero = jnp.zeros((8, 128), F32)
    acc = [[zero] * 3 for _ in range(3)]

    def put(level, value, at, width, start):
        inside = (lane >= at) & (lane < at + width)
        for turn in range(3):
            moved = pltpu.roll(value, (at - start - width * turn) % 128, 1)
            acc[level][turn] = jnp.where(inside, moved, acc[level][turn])

    for at in range(N_NEAR):
        d = (at % 2 * 2) ^ side | at // 2
        put(0, block(d, mine), at * 32, 32, 0)
        for slot, step in enumerate((0, 2, 1, 3)):
            put(1, block(d, mine ^ step), at * 32 + slot * 8, 8, 96)
        for peer in range(N_FAR):
            put(2, block(d, peer ^ ROOT_ROWS), at * 32 + peer * 2, 2, 120)
    for level in range(3):
        for turn in range(3):
            line_ref[turn * 8 : turn * 8 + 8, level * 128 : level * 128 + 128] = acc[level][turn]

    for pair in range(PAIRS):
        queries = gathered(q_ref, near_ref, back_ref, 2, pair)
        grads = gathered(g_ref, near_ref, back_ref, 3, pair)
        scores = dot_t(stacked(k_ref[:, lanes(pair)]), queries) * SCALE
        grad_probs = dot_t(stacked(v_ref[:, lanes(pair)]), grads)
        live = [None] + [chosen(off_ref, pair, level, row) for level in range(1, 4)]
        probs, grad_scores = [], []
        for side in range(2):
            head = 2 * pair + side
            rows = slice(side * TOK, side * TOK + TOK)
            probs_row, grad_row = [], []
            for level in range(4):
                cols = slice(level * 128, level * 128 + 128)
                if level == 0:
                    log_line = own_ref[2 * head : 2 * head + 1, :]
                    delta_line = own_ref[2 * head + 1 : 2 * head + 2, :]
                else:
                    at = slice(level * 128 - 128, level * 128)
                    log_line = line_ref[2 * head : 2 * head + 1, at]
                    delta_line = line_ref[2 * head + 1 : 2 * head + 2, at]
                power = scores[rows, cols] - log_line
                if level:
                    power = jnp.where(live[level][rows], power, NEG)
                prob = jnp.exp(power)
                probs_row.append(prob.astype(BF16))
                grad_row.append((prob * (grad_probs[rows, cols] - delta_line)).astype(BF16))
            probs.append(jnp.concatenate(probs_row, 1))
            grad_scores.append(jnp.concatenate(grad_row, 1))
        gv_ref[:, lanes(pair)] = halves(dot(jnp.concatenate(probs, 0), grads)).astype(BF16)
        gk_ref[:, lanes(pair)] = halves(
            dot(jnp.concatenate(grad_scores, 0), queries) * SCALE
        ).astype(BF16)


def shape(*dims, dtype=BF16):
    return jax.ShapeDtypeStruct(dims, dtype)


def cost(flops, moved, exps=0):
    return pl.CostEstimate(flops=flops, bytes_accessed=moved, transcendentals=exps)


def to_far(value, root):
    order = [[peer ^ root for peer in range(N_FAR)]]
    return lax.all_to_all(value, FAR, 0, 0, tiled=True, axis_index_groups=order)


def to_near(value):
    return lax.all_gather(value, NEAR, axis=0, tiled=True)


def to_pair(value):
    other = lax.ppermute(value, "zl", [(0, 1), (1, 0)])
    return lax.all_gather(jnp.concatenate([value, other], 0), "c", axis=0, tiled=True)


def swap_mid(value, step):
    return lax.ppermute(value, "zm", [(i, i ^ step) for i in range(4)])


def on_device(queries, key_states, value_states, grad_output, head_offsets):
    mine = (lax.axis_index("yh") * 2 + lax.axis_index("zh")) * 4 + lax.axis_index("zm")
    place = jnp.stack([mine, lax.axis_index("zl")])
    own = (key_states, value_states, queries, grad_output)
    near, mid, far = pl.pallas_call(
        pick_kernel,
        name="pick",
        out_shape=(shape(128, FULL), shape(32, FULL), shape(8 * N_FAR, FULL)),
        in_specs=[SMEM] + [pl.BlockSpec(memory_space=pl.ANY)] * 4,
        out_specs=(VMEM,) * 3,
        scratch_shapes=[pltpu.VMEM((4, TOK, FULL), BF16), pltpu.SemaphoreType.DMA((4, CUTS))],
        compiler_params=pltpu.CompilerParams(vmem_limit_bytes=62 * 1024 * 1024),
        cost_estimate=cost(200_000_000, 1_100_000),
    )(head_offsets, *own)
    far_rows = to_far(far, ROOT_ROWS)
    mid_rows = jnp.concatenate([mid, swap_mid(mid, 2), swap_mid(mid, 1), swap_mid(mid, 3)], 0)
    near_rows = to_pair(near)
    kv_rows, qg_rows = pl.pallas_call(
        split_kernel,
        name="split",
        out_shape=(shape(128, FULL), shape(128, FULL)),
        in_specs=[VMEM] * 4,
        out_specs=(VMEM,) * 2,
        compiler_params=PARAMS,
        cost_estimate=cost(100_000_000, 800_000),
    )(far_rows, mid_rows, queries, grad_output)
    kv_rows = to_pair(kv_rows)
    stats = pl.pallas_call(
        stat_kernel,
        name="stats",
        out_shape=shape(8 * N_FAR, 128, dtype=F32),
        in_specs=[SMEM] + [VMEM] * 7,
        out_specs=VMEM,
        compiler_params=PARAMS,
        cost_estimate=cost(200_000_000, 2_000_000, 300_000),
    )(head_offsets, key_states, value_states, near, mid, far, near_rows, kv_rows)
    attended, grad_query, own_stats = pl.pallas_call(
        forward_kernel,
        name="forward",
        out_shape=(
            shape(TOK, FULL),
            shape(TOK, FULL),
            shape(2 * HEADS, 128, dtype=F32),
        ),
        in_specs=[SMEM] + [VMEM] * 6,
        out_specs=(VMEM,) * 3,
        compiler_params=PARAMS,
        cost_estimate=cost(1_000_000_000, 3_000_000, 800_000),
    )(head_offsets, *own, near_rows, kv_rows)
    all_stats = to_near(to_far(stats, ROOT_STATS))
    qg_rows = to_pair(qg_rows)
    grad_key, grad_value = pl.pallas_call(
        backward_kernel,
        name="backward",
        out_shape=(shape(TOK, FULL), shape(TOK, FULL)),
        in_specs=[SMEM] * 2 + [VMEM] * 8,
        out_specs=(VMEM,) * 2,
        scratch_shapes=[pltpu.VMEM((2 * HEADS, 3 * 128), F32)],
        compiler_params=PARAMS,
        cost_estimate=cost(1_000_000_000, 3_000_000, 800_000),
    )(head_offsets, place, *own, near_rows, qg_rows, own_stats, all_stats)
    return attended, grad_query, grad_key, grad_value


def solution(mesh):
    names = tuple(name for name, _ in PARTS)
    sizes = tuple(size for _, size in PARTS)
    parts = Mesh(mesh.devices.reshape(sizes + mesh.devices.shape[1:]), names + ("dp",))
    rows = P(("dp",) + names, None)
    return jax.shard_map(
        on_device,
        mesh=parts,
        in_specs=(rows,) * 4 + (P(),),
        out_specs=(rows,) * 4,
        check_vma=False,
    )
```

```python
import functools

import jax
import jax.numpy as jnp
from jax import lax
from jax.experimental import pallas as pl
from jax.experimental.pallas import tpu as pltpu
from jax.sharding import Mesh, PartitionSpec as P

HEADS = 12
WIDTH = 64
TOK = 128
FULL = HEADS * WIDTH
PAIRS = HEADS // 2
SCALE = WIDTH ** -0.5
GROUPS = (1, 4, 16, 64)
PARTS = (("yh", 2), ("zh", 2), ("zm", 4), ("zl", 2), ("c", 2))
FAR = ("yh", "zh", "zm")
NEAR = ("zl", "c")
N_FAR = 16
N_NEAR = 4
ROWS1, ROWS2, ROWS3 = 32, 8, 2
NEG = -1e30
STAGED = 6
STAGED_FORWARD = 3
CUTS = 4
ROOT_ROWS, ROOT_STATS = 13, 3
F32 = jnp.float32
BF16 = jnp.bfloat16
VMEM = pl.BlockSpec(memory_space=pltpu.VMEM)
SMEM = pl.BlockSpec(memory_space=pltpu.SMEM)
PARAMS = pltpu.CompilerParams(vmem_limit_bytes=48 * 1024 * 1024)


def iota(shape, dim):
    return lax.broadcasted_iota(jnp.int32, shape, dim)


def dot(a, b):
    return lax.dot_general(a, b, (((1,), (0,)), ((), ())), preferred_element_type=F32)


def dot_t(a, b):
    return lax.dot_general(a, b, (((1,), (1,)), ((), ())), preferred_element_type=F32)


def lanes(pair):
    return slice(pair * 128, (pair + 1) * 128)


def halves(value):
    n = value.shape[0] // 2
    return jnp.where(iota((n, 128), 1) < WIDTH, value[:n], value[n:])


def stacked(value):
    low = iota(value.shape, 1) < WIDTH
    zero = jnp.zeros_like(value)
    return jnp.concatenate([jnp.where(low, value, zero), jnp.where(low, zero, value)], 0)


def pick_kernel(off_ref, k_hbm, v_hbm, q_hbm, g_hbm, near_ref, mid_ref, far_ref, refs, sems):
    copies = []
    for array, source in enumerate((k_hbm, v_hbm, q_hbm, g_hbm)):
        for part in range(CUTS):
            rows = pl.ds(part * (TOK // CUTS), TOK // CUTS)
            copies.append(
                pltpu.make_async_copy(
                    source.at[rows], refs.at[array, rows], sems.at[array, part]
                )
            )
    for copy in copies:
        copy.start()
    row = iota((48, TOK), 0)
    tok = iota((48, TOK), 1)
    base = jnp.where(row < 32, row * 4, jnp.where(row < 40, (row - 32) * 16, (row % 2) * 64))

    def selector(head, array):
        off = jnp.where(
            row < 32, off_ref[1, head], jnp.where(row < 40, off_ref[2, head], off_ref[3, head])
        )
        live = (row < 40) | ((row - 40) // 2 == array)
        return jnp.where((tok == base + off) & live, 1.0, 0.0).astype(BF16)

    far = [None] * PAIRS
    for first in (0, 2):
        for copy in copies[first * CUTS : (first + 2) * CUTS]:
            copy.wait()
        for pair in range(PAIRS):
            picked = []
            for array in (first, first + 1):
                choose = jnp.concatenate(
                    [selector(2 * pair, array), selector(2 * pair + 1, array)], 0
                )
                picked.append(halves(dot(choose, refs[array, :, lanes(pair)])))
            near_ref[first * 32 : first * 32 + 64, lanes(pair)] = jnp.concatenate(
                [x[:32] for x in picked], 0
            ).astype(BF16)
            mid_ref[first * 8 : first * 8 + 16, lanes(pair)] = jnp.concatenate(
                [x[32:40] for x in picked], 0
            ).astype(BF16)
            both = picked[0][40:] + picked[1][40:]
            far[pair] = both if far[pair] is None else far[pair] + both
    for pair in range(PAIRS):
        far_ref[:, lanes(pair)] = jnp.concatenate([far[pair]] * N_FAR, 0).astype(BF16)


def split_kernel(far_ref, mid_ref, q_ref, g_ref, kv_ref, qg_ref):
    del q_ref, g_ref
    both = jnp.concatenate([far_ref[...], mid_ref[...]], 0)
    row = iota((128, 256), 0)
    col = iota((128, 256), 1)
    run = row // 32
    slot = row % 32
    for first, out_ref in ((0, kv_ref), (2, qg_ref)):
        array = first + run // 2
        far_col = slot // 2 * 8 + array * 2 + slot % 2
        mid_col = 128 + slot // 8 * 32 + array * 8 + slot % 8
        choose = jnp.where(col == jnp.where(run % 2 == 0, far_col, mid_col), 1.0, 0.0)
        out_ref[...] = dot(choose.astype(BF16), both).astype(BF16)


def gathered(own_ref, near_ref, back_ref, array, pair):
    cols = lanes(pair)
    one = [near_ref[d * 128 + array * 32 : d * 128 + array * 32 + 32, cols] for d in range(N_NEAR)]
    half = (array % 2) * 64
    three = [back_ref[d * 128 + half : d * 128 + half + 32, cols] for d in range(N_NEAR)]
    two = [back_ref[d * 128 + half + 32 : d * 128 + half + 64, cols] for d in range(N_NEAR)]
    return jnp.concatenate([own_ref[:, cols]] + one + two + three, 0)


def chosen(off_ref, pair, level, tok):
    half = tok.shape[0] // 2
    off = jnp.where(
        iota(tok.shape, 0) < half, off_ref[level, 2 * pair], off_ref[level, 2 * pair + 1]
    )
    return (tok & (GROUPS[level] - 1)) == off


def softmax(scores, live):
    blocks = [scores[:, level * 128 : level * 128 + 128] for level in range(4)]
    for level in range(1, 4):
        blocks[level] = jnp.where(live[level - 1], blocks[level], NEG)
    top = jnp.maximum(jnp.maximum(blocks[0], blocks[1]), jnp.maximum(blocks[2], blocks[3]))
    top = jnp.max(top, axis=1, keepdims=True)
    raw = [jnp.exp(block - top) for block in blocks]
    total = jnp.sum((raw[0] + raw[1]) + (raw[2] + raw[3]), axis=1, keepdims=True)
    return jnp.concatenate(raw, 1), total, top


def stat_kernel(
    off_ref, k_ref, v_ref, near_ref, mid_ref, far_ref, near_rows_ref, back_ref, stat_ref
):
    row = iota((48, 1), 0)
    both = iota((96, 128), 0)
    slot = jnp.where(both < 48, both, both - 48)
    sums = [None] * 8

    def pick(level, pair):
        return jnp.where(both < 48, off_ref[level, 2 * pair], off_ref[level, 2 * pair + 1])

    def scores_of(pair):
        cols = lanes(pair)
        far = far_ref[:16, cols].astype(F32)[:8]
        mid = mid_ref[16:, cols].astype(F32)
        near = near_ref[64:, cols].astype(F32)
        query = jnp.concatenate([near[:32], mid[:8], pltpu.roll(far, 4, 0)], 0).astype(BF16)
        grad = stacked(jnp.concatenate([near[32:], mid[8:], pltpu.roll(far, 2, 0)], 0))
        keys = gathered(k_ref, near_rows_ref, back_ref, 0, pair)
        return dot_t(stacked(query), keys) * SCALE, grad

    def weights_of(pair, scores):
        tok = jnp.where(
            slot < 32,
            slot * 4 + pick(1, pair),
            jnp.where(slot < 40, (slot - 32) * 16 + pick(2, pair), slot % 2 * 64 + pick(3, pair)),
        )
        live = [chosen(off_ref, pair, level, tok) for level in range(1, 4)]
        raw, total, top = softmax(scores, live)
        return raw.astype(BF16), total, top

    def columns_of(pair, grad, raw, total, top):
        values = gathered(v_ref, near_rows_ref, back_ref, 1, pair)
        out = (dot(raw, values) * (1.0 / total)).astype(BF16).astype(F32)
        return top + jnp.log(total), jnp.sum(grad * out, axis=1, keepdims=True)

    for first in range(0, PAIRS, STAGED):
        pairs = range(first, first + STAGED)
        scores = [scores_of(pair) for pair in pairs]
        weights = [weights_of(pair, part[0]) for pair, part in zip(pairs, scores)]
        columns = [
            columns_of(pair, part[1], *weight)
            for pair, part, weight in zip(pairs, scores, weights)
        ]
        for pair, (logs, delta) in zip(pairs, columns):
            turn = pair // 2
            lane = jnp.where(
                row < 32,
                row + 32 * turn,
                jnp.where(
                    row < 40, row + 64 + 8 * turn, jnp.where(row < 42, row + 80 + 2 * turn, -1)
                ),
            )
            hit = iota((48, 128), 1) == lane
            for side in range(2):
                for kind, column in enumerate((logs, delta)):
                    line = jnp.sum(
                        jnp.where(hit, column[side * 48 : side * 48 + 48], 0.0),
                        axis=0,
                        keepdims=True,
                    )
                    place = 2 * ((2 * pair + side) % 4) + kind
                    sums[place] = line if sums[place] is None else sums[place] + line
    stat_ref[...] = jnp.concatenate(sums * N_FAR, 0)


def forward_kernel(
    off_ref, k_ref, v_ref, q_ref, g_ref, near_ref, back_ref, att_ref, gq_ref, own_ref
):
    eye = iota((TOK, 128), 0) == iota((TOK, 128), 1)
    row = iota((2 * TOK, 128), 0)
    def products(pair):
        keys = gathered(k_ref, near_ref, back_ref, 0, pair)
        values = gathered(v_ref, near_ref, back_ref, 1, pair)
        grad = stacked(g_ref[:, lanes(pair)])
        scores = dot_t(stacked(q_ref[:, lanes(pair)]), keys) * SCALE
        return keys, values, grad, scores

    def weights(pair, scores):
        return softmax(scores, [chosen(off_ref, pair, level, row) for level in range(1, 4)])

    def outputs(pair, values, grad, raw, total):
        inverse = 1.0 / total
        out = halves(dot(raw.astype(BF16), values) * inverse).astype(BF16)
        att_ref[:, lanes(pair)] = out
        out = out.astype(F32)
        delta = jnp.sum(grad.astype(F32) * jnp.concatenate([out, out], 0), axis=1, keepdims=True)
        grad_probs = dot_t(grad, values)
        return delta, (raw * inverse * (grad_probs - delta)).astype(BF16)

    for first in range(0, PAIRS, STAGED_FORWARD):
        pairs = range(first, first + STAGED_FORWARD)
        parts = [products(pair) for pair in pairs]
        soft = [weights(pair, part[3]) for pair, part in zip(pairs, parts)]
        done = [
            outputs(pair, part[1], part[2], raw, total)
            for pair, part, (raw, total, _) in zip(pairs, parts, soft)
        ]
        for pair, part, (_, total, top), (delta, grad_scores) in zip(pairs, parts, soft, done):
            gq_ref[:, lanes(pair)] = halves(dot(grad_scores, part[0]) * SCALE).astype(BF16)
            logs = top + jnp.log(total)
            for side in range(2):
                head = 2 * pair + side
                for kind, column in enumerate((logs, delta)):
                    own_ref[2 * head + kind : 2 * head + kind + 1, :] = jnp.sum(
                        jnp.where(eye, column[side * TOK : side * TOK + TOK], 0.0),
                        axis=0,
                        keepdims=True,
                    )


def backward_kernel(
    off_ref, where_ref, k_ref, v_ref, q_ref, g_ref, near_ref, back_ref, own_ref, stat_ref,
    gk_ref, gv_ref, line_ref,
):
    lane = iota((8, 128), 1)
    row = iota((2 * TOK, 128), 0)
    mine = where_ref[0]
    side = where_ref[1] * 2

    def block(d, peer):
        return stat_ref[pl.ds(pl.multiple_of((d * N_FAR + (peer ^ ROOT_STATS)) * 8, 8), 8), :]

    zero = jnp.zeros((8, 128), F32)
    acc = [[zero] * 3 for _ in range(3)]

    def put(level, value, at, width, start):
        inside = (lane >= at) & (lane < at + width)
        for turn in range(3):
            moved = pltpu.roll(value, (at - start - width * turn) % 128, 1)
            acc[level][turn] = jnp.where(inside, moved, acc[level][turn])

    for at in range(N_NEAR):
        d = (at % 2 * 2) ^ side | at // 2
        put(0, block(d, mine), at * 32, 32, 0)
        for slot, step in enumerate((0, 2, 1, 3)):
            put(1, block(d, mine ^ step), at * 32 + slot * 8, 8, 96)
        for peer in range(N_FAR):
            put(2, block(d, peer ^ ROOT_ROWS), at * 32 + peer * 2, 2, 120)
    for level in range(3):
        for turn in range(3):
            line_ref[turn * 8 : turn * 8 + 8, level * 128 : level * 128 + 128] = acc[level][turn]

    for pair in range(PAIRS):
        queries = gathered(q_ref, near_ref, back_ref, 2, pair)
        grads = gathered(g_ref, near_ref, back_ref, 3, pair)
        scores = dot_t(stacked(k_ref[:, lanes(pair)]), queries) * SCALE
        grad_probs = dot_t(stacked(v_ref[:, lanes(pair)]), grads)
        live = [None] + [chosen(off_ref, pair, level, row) for level in range(1, 4)]
        probs, grad_scores = [], []
        for side in range(2):
            head = 2 * pair + side
            rows = slice(side * TOK, side * TOK + TOK)
            probs_row, grad_row = [], []
            for level in range(4):
                cols = slice(level * 128, level * 128 + 128)
                if level == 0:
                    log_line = own_ref[2 * head : 2 * head + 1, :]
                    delta_line = own_ref[2 * head + 1 : 2 * head + 2, :]
                else:
                    at = slice(level * 128 - 128, level * 128)
                    log_line = line_ref[2 * head : 2 * head + 1, at]
                    delta_line = line_ref[2 * head + 1 : 2 * head + 2, at]
                power = scores[rows, cols] - log_line
                if level:
                    power = jnp.where(live[level][rows], power, NEG)
                prob = jnp.exp(power)
                probs_row.append(prob.astype(BF16))
                grad_row.append((prob * (grad_probs[rows, cols] - delta_line)).astype(BF16))
            probs.append(jnp.concatenate(probs_row, 1))
            grad_scores.append(jnp.concatenate(grad_row, 1))
        gv_ref[:, lanes(pair)] = halves(dot(jnp.concatenate(probs, 0), grads)).astype(BF16)
        gk_ref[:, lanes(pair)] = halves(
            dot(jnp.concatenate(grad_scores, 0), queries) * SCALE
        ).astype(BF16)


def shape(*dims, dtype=BF16):
    return jax.ShapeDtypeStruct(dims, dtype)


def cost(flops, moved, exps=0):
    return pl.CostEstimate(flops=flops, bytes_accessed=moved, transcendentals=exps)


def to_far(value, root):
    order = [[peer ^ root for peer in range(N_FAR)]]
    return lax.all_to_all(value, FAR, 0, 0, tiled=True, axis_index_groups=order)


def to_near(value):
    return lax.all_gather(value, NEAR, axis=0, tiled=True)


def to_pair(value):
    other = lax.ppermute(value, "zl", [(0, 1), (1, 0)])
    return lax.all_gather(jnp.concatenate([value, other], 0), "c", axis=0, tiled=True)


def swap_mid(value, step):
    return lax.ppermute(value, "zm", [(i, i ^ step) for i in range(4)])


def on_device(queries, key_states, value_states, grad_output, head_offsets):
    mine = (lax.axis_index("yh") * 2 + lax.axis_index("zh")) * 4 + lax.axis_index("zm")
    place = jnp.stack([mine, lax.axis_index("zl")])
    own = (key_states, value_states, queries, grad_output)
    near, mid, far = pl.pallas_call(
        pick_kernel,
        name="pick",
        out_shape=(shape(128, FULL), shape(32, FULL), shape(8 * N_FAR, FULL)),
        in_specs=[SMEM] + [pl.BlockSpec(memory_space=pl.ANY)] * 4,
        out_specs=(VMEM,) * 3,
        scratch_shapes=[pltpu.VMEM((4, TOK, FULL), BF16), pltpu.SemaphoreType.DMA((4, CUTS))],
        compiler_params=pltpu.CompilerParams(vmem_limit_bytes=62 * 1024 * 1024),
        cost_estimate=cost(200_000_000, 1_100_000),
    )(head_offsets, *own)
    far_rows = to_far(far, ROOT_ROWS)
    mid_rows = jnp.concatenate([mid, swap_mid(mid, 2), swap_mid(mid, 1), swap_mid(mid, 3)], 0)
    near_rows = to_pair(near)
    kv_rows, qg_rows = pl.pallas_call(
        split_kernel,
        name="split",
        out_shape=(shape(128, FULL), shape(128, FULL)),
        in_specs=[VMEM] * 4,
        out_specs=(VMEM,) * 2,
        compiler_params=PARAMS,
        cost_estimate=cost(100_000_000, 800_000),
    )(far_rows, mid_rows, queries, grad_output)
    kv_rows = to_pair(kv_rows)
    stats = pl.pallas_call(
        stat_kernel,
        name="stats",
        out_shape=shape(8 * N_FAR, 128, dtype=F32),
        in_specs=[SMEM] + [VMEM] * 7,
        out_specs=VMEM,
        compiler_params=PARAMS,
        cost_estimate=cost(200_000_000, 2_000_000, 300_000),
    )(head_offsets, key_states, value_states, near, mid, far, near_rows, kv_rows)
    attended, grad_query, own_stats = pl.pallas_call(
        forward_kernel,
        name="forward",
        out_shape=(
            shape(TOK, FULL),
            shape(TOK, FULL),
            shape(2 * HEADS, 128, dtype=F32),
        ),
        in_specs=[SMEM] + [VMEM] * 6,
        out_specs=(VMEM,) * 3,
        compiler_params=PARAMS,
        cost_estimate=cost(1_000_000_000, 3_000_000, 800_000),
    )(head_offsets, *own, near_rows, kv_rows)
    all_stats = to_near(to_far(stats, ROOT_STATS))
    qg_rows = to_pair(qg_rows)
    grad_key, grad_value = pl.pallas_call(
        backward_kernel,
        name="backward",
        out_shape=(shape(TOK, FULL), shape(TOK, FULL)),
        in_specs=[SMEM] * 2 + [VMEM] * 8,
        out_specs=(VMEM,) * 2,
        scratch_shapes=[pltpu.VMEM((2 * HEADS, 3 * 128), F32)],
        compiler_params=PARAMS,
        cost_estimate=cost(1_000_000_000, 3_000_000, 800_000),
    )(head_offsets, place, *own, near_rows, qg_rows, own_stats, all_stats)
    return attended, grad_query, grad_key, grad_value


def solution(mesh):
    names = tuple(name for name, _ in PARTS)
    sizes = tuple(size for _, size in PARTS)
    parts = Mesh(mesh.devices.reshape(sizes + mesh.devices.shape[1:]), names + ("dp",))
    rows = P(("dp",) + names, None)
    return jax.shard_map(
        on_device,
        mesh=parts,
        in_specs=(rows,) * 4 + (P(),),
        out_specs=(rows,) * 4,
        check_vma=False,
    )
```

```python
import functools

import jax
import jax.numpy as jnp
from jax import lax
from jax.experimental import pallas as pl
from jax.experimental.pallas import tpu as pltpu
from jax.sharding import Mesh, PartitionSpec as P

HEADS = 12
WIDTH = 64
TOK = 128
FULL = HEADS * WIDTH
PAIRS = HEADS // 2
SCALE = WIDTH ** -0.5
GROUPS = (1, 4, 16, 64)
PARTS = (("yh", 2), ("zh", 2), ("zm", 4), ("zl", 2), ("c", 2))
FAR = ("yh", "zh", "zm")
NEAR = ("zl", "c")
N_FAR = 16
N_NEAR = 4
ROWS1, ROWS2, ROWS3 = 32, 8, 2
NEG = -1e30
STAGED = 6
STAGED_FORWARD = 3
CUTS = 1
ROOT_ROWS, ROOT_STATS = 13, 4
F32 = jnp.float32
BF16 = jnp.bfloat16
VMEM = pl.BlockSpec(memory_space=pltpu.VMEM)
SMEM = pl.BlockSpec(memory_space=pltpu.SMEM)
PARAMS = pltpu.CompilerParams(vmem_limit_bytes=48 * 1024 * 1024)


def iota(shape, dim):
    return lax.broadcasted_iota(jnp.int32, shape, dim)


def dot(a, b):
    return lax.dot_general(a, b, (((1,), (0,)), ((), ())), preferred_element_type=F32)


def dot_t(a, b):
    return lax.dot_general(a, b, (((1,), (1,)), ((), ())), preferred_element_type=F32)


def lanes(pair):
    return slice(pair * 128, (pair + 1) * 128)


def halves(value):
    n = value.shape[0] // 2
    return jnp.where(iota((n, 128), 1) < WIDTH, value[:n], value[n:])


def stacked(value):
    low = iota(value.shape, 1) < WIDTH
    zero = jnp.zeros_like(value)
    return jnp.concatenate([jnp.where(low, value, zero), jnp.where(low, zero, value)], 0)


def pick_kernel(off_ref, k_hbm, v_hbm, q_hbm, g_hbm, near_ref, mid_ref, far_ref, refs, sems):
    copies = []
    for array, source in enumerate((k_hbm, v_hbm, q_hbm, g_hbm)):
        for part in range(CUTS):
            rows = pl.ds(part * (TOK // CUTS), TOK // CUTS)
            copies.append(
                pltpu.make_async_copy(
                    source.at[rows], refs.at[array, rows], sems.at[array, part]
                )
            )
    for copy in copies:
        copy.start()
    row = iota((48, TOK), 0)
    tok = iota((48, TOK), 1)
    base = jnp.where(row < 32, row * 4, jnp.where(row < 40, (row - 32) * 16, (row % 2) * 64))

    def selector(head, array):
        off = jnp.where(
            row < 32, off_ref[1, head], jnp.where(row < 40, off_ref[2, head], off_ref[3, head])
        )
        live = (row < 40) | ((row - 40) // 2 == array)
        return jnp.where((tok == base + off) & live, 1.0, 0.0).astype(BF16)

    far = [None] * PAIRS
    for first in (0, 2):
        for copy in copies[first * CUTS : (first + 2) * CUTS]:
            copy.wait()
        for pair in range(PAIRS):
            picked = []
            for array in (first, first + 1):
                choose = jnp.concatenate(
                    [selector(2 * pair, array), selector(2 * pair + 1, array)], 0
                )
                picked.append(halves(dot(choose, refs[array, :, lanes(pair)])))
            near_ref[first * 32 : first * 32 + 64, lanes(pair)] = jnp.concatenate(
                [x[:32] for x in picked], 0
            ).astype(BF16)
            mid_ref[first * 8 : first * 8 + 16, lanes(pair)] = jnp.concatenate(
                [x[32:40] for x in picked], 0
            ).astype(BF16)
            both = picked[0][40:] + picked[1][40:]
            far[pair] = both if far[pair] is None else far[pair] + both
    for pair in range(PAIRS):
        far_ref[:, lanes(pair)] = jnp.concatenate([far[pair]] * N_FAR, 0).astype(BF16)


def split_kernel(far_ref, mid_ref, q_ref, g_ref, kv_ref, qg_ref):
    del q_ref, g_ref
    both = jnp.concatenate([far_ref[...], mid_ref[...]], 0)
    row = iota((128, 256), 0)
    col = iota((128, 256), 1)
    run = row // 32
    slot = row % 32
    for first, out_ref in ((0, kv_ref), (2, qg_ref)):
        array = first + run // 2
        far_col = slot // 2 * 8 + array * 2 + slot % 2
        mid_col = 128 + slot // 8 * 32 + array * 8 + slot % 8
        choose = jnp.where(col == jnp.where(run % 2 == 0, far_col, mid_col), 1.0, 0.0)
        out_ref[...] = dot(choose.astype(BF16), both).astype(BF16)


def gathered(own_ref, near_ref, back_ref, array, pair):
    cols = lanes(pair)
    one = [near_ref[d * 128 + array * 32 : d * 128 + array * 32 + 32, cols] for d in range(N_NEAR)]
    half = (array % 2) * 64
    three = [back_ref[d * 128 + half : d * 128 + half + 32, cols] for d in range(N_NEAR)]
    two = [back_ref[d * 128 + half + 32 : d * 128 + half + 64, cols] for d in range(N_NEAR)]
    return jnp.concatenate([own_ref[:, cols]] + one + two + three, 0)


def chosen(off_ref, pair, level, tok):
    half = tok.shape[0] // 2
    off = jnp.where(
        iota(tok.shape, 0) < half, off_ref[level, 2 * pair], off_ref[level, 2 * pair + 1]
    )
    return (tok & (GROUPS[level] - 1)) == off


def softmax(scores, live):
    blocks = [scores[:, level * 128 : level * 128 + 128] for level in range(4)]
    for level in range(1, 4):
        blocks[level] = jnp.where(live[level - 1], blocks[level], NEG)
    top = jnp.maximum(jnp.maximum(blocks[0], blocks[1]), jnp.maximum(blocks[2], blocks[3]))
    top = jnp.max(top, axis=1, keepdims=True)
    raw = [jnp.exp(block - top) for block in blocks]
    total = jnp.sum((raw[0] + raw[1]) + (raw[2] + raw[3]), axis=1, keepdims=True)
    return jnp.concatenate(raw, 1), total, top


def stat_kernel(
    off_ref, k_ref, v_ref, near_ref, mid_ref, far_ref, near_rows_ref, back_ref, stat_ref
):
    row = iota((48, 1), 0)
    both = iota((96, 128), 0)
    slot = jnp.where(both < 48, both, both - 48)
    sums = [None] * 8

    def pick(level, pair):
        return jnp.where(both < 48, off_ref[level, 2 * pair], off_ref[level, 2 * pair + 1])

    def scores_of(pair):
        cols = lanes(pair)
        far = far_ref[:16, cols].astype(F32)[:8]
        mid = mid_ref[16:, cols].astype(F32)
        near = near_ref[64:, cols].astype(F32)
        query = jnp.concatenate([near[:32], mid[:8], pltpu.roll(far, 4, 0)], 0).astype(BF16)
        grad = stacked(jnp.concatenate([near[32:], mid[8:], pltpu.roll(far, 2, 0)], 0))
        keys = gathered(k_ref, near_rows_ref, back_ref, 0, pair)
        return dot_t(stacked(query), keys) * SCALE, grad

    def weights_of(pair, scores):
        tok = jnp.where(
            slot < 32,
            slot * 4 + pick(1, pair),
            jnp.where(slot < 40, (slot - 32) * 16 + pick(2, pair), slot % 2 * 64 + pick(3, pair)),
        )
        live = [chosen(off_ref, pair, level, tok) for level in range(1, 4)]
        raw, total, top = softmax(scores, live)
        return raw.astype(BF16), total, top

    def columns_of(pair, grad, raw, total, top):
        values = gathered(v_ref, near_rows_ref, back_ref, 1, pair)
        out = (dot(raw, values) * (1.0 / total)).astype(BF16).astype(F32)
        return top + jnp.log(total), jnp.sum(grad * out, axis=1, keepdims=True)

    for first in range(0, PAIRS, STAGED):
        pairs = range(first, first + STAGED)
        scores = [scores_of(pair) for pair in pairs]
        weights = [weights_of(pair, part[0]) for pair, part in zip(pairs, scores)]
        columns = [
            columns_of(pair, part[1], *weight)
            for pair, part, weight in zip(pairs, scores, weights)
        ]
        for pair, (logs, delta) in zip(pairs, columns):
            turn = pair // 2
            lane = jnp.where(
                row < 32,
                row + 32 * turn,
                jnp.where(
                    row < 40, row + 64 + 8 * turn, jnp.where(row < 42, row + 80 + 2 * turn, -1)
                ),
            )
            hit = iota((48, 128), 1) == lane
            for side in range(2):
                for kind, column in enumerate((logs, delta)):
                    line = jnp.sum(
                        jnp.where(hit, column[side * 48 : side * 48 + 48], 0.0),
                        axis=0,
                        keepdims=True,
                    )
                    place = 2 * ((2 * pair + side) % 4) + kind
                    sums[place] = line if sums[place] is None else sums[place] + line
    stat_ref[...] = jnp.concatenate(sums * N_FAR, 0)


def forward_kernel(
    off_ref, k_ref, v_ref, q_ref, g_ref, near_ref, back_ref, att_ref, gq_ref, own_ref
):
    eye = iota((TOK, 128), 0) == iota((TOK, 128), 1)
    row = iota((2 * TOK, 128), 0)
    def products(pair):
        keys = gathered(k_ref, near_ref, back_ref, 0, pair)
        values = gathered(v_ref, near_ref, back_ref, 1, pair)
        grad = stacked(g_ref[:, lanes(pair)])
        scores = dot_t(stacked(q_ref[:, lanes(pair)]), keys) * SCALE
        return keys, values, grad, scores

    def weights(pair, scores):
        return softmax(scores, [chosen(off_ref, pair, level, row) for level in range(1, 4)])

    def outputs(pair, values, grad, raw, total):
        inverse = 1.0 / total
        out = halves(dot(raw.astype(BF16), values) * inverse).astype(BF16)
        att_ref[:, lanes(pair)] = out
        out = out.astype(F32)
        delta = jnp.sum(grad.astype(F32) * jnp.concatenate([out, out], 0), axis=1, keepdims=True)
        grad_probs = dot_t(grad, values)
        return delta, (raw * inverse * (grad_probs - delta)).astype(BF16)

    for first in range(0, PAIRS, STAGED_FORWARD):
        pairs = range(first, first + STAGED_FORWARD)
        parts = [products(pair) for pair in pairs]
        soft = [weights(pair, part[3]) for pair, part in zip(pairs, parts)]
        done = [
            outputs(pair, part[1], part[2], raw, total)
            for pair, part, (raw, total, _) in zip(pairs, parts, soft)
        ]
        for pair, part, (_, total, top), (delta, grad_scores) in zip(pairs, parts, soft, done):
            gq_ref[:, lanes(pair)] = halves(dot(grad_scores, part[0]) * SCALE).astype(BF16)
            logs = top + jnp.log(total)
            for side in range(2):
                head = 2 * pair + side
                for kind, column in enumerate((logs, delta)):
                    own_ref[2 * head + kind : 2 * head + kind + 1, :] = jnp.sum(
                        jnp.where(eye, column[side * TOK : side * TOK + TOK], 0.0),
                        axis=0,
                        keepdims=True,
                    )


def backward_kernel(
    off_ref, where_ref, k_ref, v_ref, q_ref, g_ref, near_ref, back_ref, own_ref, stat_ref,
    gk_ref, gv_ref, line_ref,
):
    lane = iota((8, 128), 1)
    row = iota((2 * TOK, 128), 0)
    mine = where_ref[0]
    side = where_ref[1] * 2

    def block(d, peer):
        return stat_ref[pl.ds(pl.multiple_of((d * N_FAR + (peer ^ ROOT_STATS)) * 8, 8), 8), :]

    zero = jnp.zeros((8, 128), F32)
    acc = [[zero] * 3 for _ in range(3)]

    def put(level, value, at, width, start):
        inside = (lane >= at) & (lane < at + width)
        for turn in range(3):
            moved = pltpu.roll(value, (at - start - width * turn) % 128, 1)
            acc[level][turn] = jnp.where(inside, moved, acc[level][turn])

    for at in range(N_NEAR):
        d = (at % 2 * 2) ^ side | at // 2
        put(0, block(d, mine), at * 32, 32, 0)
        for slot, step in enumerate((0, 2, 1, 3)):
            put(1, block(d, mine ^ step), at * 32 + slot * 8, 8, 96)
        for peer in range(N_FAR):
            put(2, block(d, peer ^ ROOT_ROWS), at * 32 + peer * 2, 2, 120)
    for level in range(3):
        for turn in range(3):
            line_ref[turn * 8 : turn * 8 + 8, level * 128 : level * 128 + 128] = acc[level][turn]

    for pair in range(PAIRS):
        queries = gathered(q_ref, near_ref, back_ref, 2, pair)
        grads = gathered(g_ref, near_ref, back_ref, 3, pair)
        scores = dot_t(stacked(k_ref[:, lanes(pair)]), queries) * SCALE
        grad_probs = dot_t(stacked(v_ref[:, lanes(pair)]), grads)
        live = [None] + [chosen(off_ref, pair, level, row) for level in range(1, 4)]
        probs, grad_scores = [], []
        for side in range(2):
            head = 2 * pair + side
            rows = slice(side * TOK, side * TOK + TOK)
            probs_row, grad_row = [], []
            for level in range(4):
                cols = slice(level * 128, level * 128 + 128)
                if level == 0:
                    log_line = own_ref[2 * head : 2 * head + 1, :]
                    delta_line = own_ref[2 * head + 1 : 2 * head + 2, :]
                else:
                    at = slice(level * 128 - 128, level * 128)
                    log_line = line_ref[2 * head : 2 * head + 1, at]
                    delta_line = line_ref[2 * head + 1 : 2 * head + 2, at]
                power = scores[rows, cols] - log_line
                if level:
                    power = jnp.where(live[level][rows], power, NEG)
                prob = jnp.exp(power)
                probs_row.append(prob.astype(BF16))
                grad_row.append((prob * (grad_probs[rows, cols] - delta_line)).astype(BF16))
            probs.append(jnp.concatenate(probs_row, 1))
            grad_scores.append(jnp.concatenate(grad_row, 1))
        gv_ref[:, lanes(pair)] = halves(dot(jnp.concatenate(probs, 0), grads)).astype(BF16)
        gk_ref[:, lanes(pair)] = halves(
            dot(jnp.concatenate(grad_scores, 0), queries) * SCALE
        ).astype(BF16)


def shape(*dims, dtype=BF16):
    return jax.ShapeDtypeStruct(dims, dtype)


def cost(flops, moved, exps=0):
    return pl.CostEstimate(flops=flops, bytes_accessed=moved, transcendentals=exps)


def to_far(value, root):
    order = [[peer ^ root for peer in range(N_FAR)]]
    return lax.all_to_all(value, FAR, 0, 0, tiled=True, axis_index_groups=order)


def to_near(value):
    return lax.all_gather(value, NEAR, axis=0, tiled=True)


def to_pair(value):
    other = lax.ppermute(value, "zl", [(0, 1), (1, 0)])
    return lax.all_gather(jnp.concatenate([value, other], 0), "c", axis=0, tiled=True)


def swap_mid(value, step):
    return lax.ppermute(value, "zm", [(i, i ^ step) for i in range(4)])


def on_device(queries, key_states, value_states, grad_output, head_offsets):
    mine = (lax.axis_index("yh") * 2 + lax.axis_index("zh")) * 4 + lax.axis_index("zm")
    place = jnp.stack([mine, lax.axis_index("zl")])
    own = (key_states, value_states, queries, grad_output)
    near, mid, far = pl.pallas_call(
        pick_kernel,
        name="pick",
        out_shape=(shape(128, FULL), shape(32, FULL), shape(8 * N_FAR, FULL)),
        in_specs=[SMEM] + [pl.BlockSpec(memory_space=pl.ANY)] * 4,
        out_specs=(VMEM,) * 3,
        scratch_shapes=[pltpu.VMEM((4, TOK, FULL), BF16), pltpu.SemaphoreType.DMA((4, CUTS))],
        compiler_params=pltpu.CompilerParams(vmem_limit_bytes=62 * 1024 * 1024),
        cost_estimate=cost(200_000_000, 1_100_000),
    )(head_offsets, *own)
    far_rows = to_far(far, ROOT_ROWS)
    mid_rows = jnp.concatenate([mid, swap_mid(mid, 2), swap_mid(mid, 1), swap_mid(mid, 3)], 0)
    near_rows = to_pair(near)
    kv_rows, qg_rows = pl.pallas_call(
        split_kernel,
        name="split",
        out_shape=(shape(128, FULL), shape(128, FULL)),
        in_specs=[VMEM] * 4,
        out_specs=(VMEM,) * 2,
        compiler_params=PARAMS,
        cost_estimate=cost(100_000_000, 800_000),
    )(far_rows, mid_rows, queries, grad_output)
    kv_rows = to_pair(kv_rows)
    stats = pl.pallas_call(
        stat_kernel,
        name="stats",
        out_shape=shape(8 * N_FAR, 128, dtype=F32),
        in_specs=[SMEM] + [VMEM] * 7,
        out_specs=VMEM,
        compiler_params=PARAMS,
        cost_estimate=cost(200_000_000, 2_000_000, 300_000),
    )(head_offsets, key_states, value_states, near, mid, far, near_rows, kv_rows)
    attended, grad_query, own_stats = pl.pallas_call(
        forward_kernel,
        name="forward",
        out_shape=(
            shape(TOK, FULL),
            shape(TOK, FULL),
            shape(2 * HEADS, 128, dtype=F32),
        ),
        in_specs=[SMEM] + [VMEM] * 6,
        out_specs=(VMEM,) * 3,
        compiler_params=PARAMS,
        cost_estimate=cost(1_000_000_000, 3_000_000, 800_000),
    )(head_offsets, *own, near_rows, kv_rows)
    all_stats = to_near(to_far(stats, ROOT_STATS))
    qg_rows = to_pair(qg_rows)
    grad_key, grad_value = pl.pallas_call(
        backward_kernel,
        name="backward",
        out_shape=(shape(TOK, FULL), shape(TOK, FULL)),
        in_specs=[SMEM] * 2 + [VMEM] * 8,
        out_specs=(VMEM,) * 2,
        scratch_shapes=[pltpu.VMEM((2 * HEADS, 3 * 128), F32)],
        compiler_params=PARAMS,
        cost_estimate=cost(1_000_000_000, 3_000_000, 800_000),
    )(head_offsets, place, *own, near_rows, qg_rows, own_stats, all_stats)
    return attended, grad_query, grad_key, grad_value


def solution(mesh):
    names = tuple(name for name, _ in PARTS)
    sizes = tuple(size for _, size in PARTS)
    parts = Mesh(mesh.devices.reshape(sizes + mesh.devices.shape[1:]), names + ("dp",))
    rows = P(("dp",) + names, None)
    return jax.shard_map(
        on_device,
        mesh=parts,
        in_specs=(rows,) * 4 + (P(),),
        out_specs=(rows,) * 4,
        check_vma=False,
    )
```
